256 devices in a mesh: seq: 32 (over x_lo, z, core), resp: 8 (over y, x_hi).
Axes of the slice: x: 4 (x_hi: 2, x_lo: 2; x = x_hi * 2 + x_lo), y: 4, z: 8, core: 2. Of those that a mesh axis runs over, the one named last changes fastest.
Arguments:
- queries: bfloat16 [8, 4096, 4096], P('resp', 'seq'), may hold values from -7 to 7
- resp_keys: bfloat16 [8, 4096, 1024], P('resp', 'seq'), may hold values from -6 to 6
- resp_values: bfloat16 [8, 4096, 1024], P('resp', 'seq'), may hold values from -6 to 6
- prompt_keys: bfloat16 [2, 1024, 1024], P(None, 'seq'), may hold values from -4 to 4
- prompt_values: bfloat16 [2, 1024, 1024], P(None, 'seq'), may hold values from -6 to 6
- response_prompt: int32 [32], replicated, may hold values from 0 to 1, as said below
- out_grad: bfloat16 [8, 4096, 4096], P('resp', 'seq'), may hold values from -6 to 6
Outputs:
- attended: bfloat16 [8, 4096, 4096], P('resp', 'seq')
- query_grad: bfloat16 [8, 4096, 4096], P('resp', 'seq')
- resp_key_grad: bfloat16 [8, 4096, 1024], P('resp', 'seq')
- resp_value_grad: bfloat16 [8, 4096, 1024], P('resp', 'seq')
- prompt_key_grad: bfloat16 [2, 1024, 1024], P(None, 'seq')
- prompt_value_grad: bfloat16 [2, 1024, 1024], P(None, 'seq')
The draws below stay inside these ranges and needn't reach their ends.
Inputs may be any that keep to these rules, and one draw needn't show every extreme that they name: `response_prompt`: each of the 2 prompts has at least one response.
All inputs are finite; a program needn't handle non-finite values.
Results may differ from the reference program's by a relative error of at most 0.0051.
Values may be sent and summed in bfloat16 or wider, within the bound.
A program may use at most 128 MiB of HBM per device.

```python
import math
import jax
import jax.numpy as jnp
from jax import lax

H = 32
KVH = 8
HD = 128
RLEN = 1024
PROMPTS = 2
PLEN = 1024
RESPONSES = 32
RROWS = 8
RTOK = 4096


def draw_queries(key, part):
    key = jax.random.fold_in(key, 11)
    shape = (RROWS, RTOK, H * HD)
    values = jnp.clip(jax.random.normal(key, shape, jnp.float32), -4.0, 4.0)
    return values.astype(jnp.bfloat16)


def draw_prompt_keys(key, part):
    key = jax.random.fold_in(key, 12)
    shape = (PROMPTS, PLEN, KVH * HD)
    values = jnp.clip(jax.random.normal(key, shape, jnp.float32), -4.0, 4.0)
    return values.astype(jnp.bfloat16)


def draw_response_prompt(key, part):
    key = jax.random.fold_in(key, 13)
    first_key, second_key = jax.random.split(key)
    second_count = jax.random.randint(first_key, (), 1, RESPONSES)
    shuffled = jax.random.permutation(second_key, RESPONSES)
    return (shuffled < second_count).astype(jnp.int32)


def level_of(own_key, shape, cuts, smallest, top_value):
    factor_of = 1.0
    for axis_at, parts in cuts:
        steps = jax.random.uniform(jax.random.fold_in(jax.random.fold_in(own_key, 6), axis_at), (parts,), jnp.float32, smallest / len(cuts), top_value / len(cuts))
        factor_of = factor_of * jnp.repeat(jnp.exp(steps), shape[axis_at] // parts).reshape((-1,) + (1,) * (len(shape) - 1 - axis_at))
    return factor_of


def centred(key, dims, deviation, most, pieces=(), dtype=jnp.bfloat16):
    factor_of = level_of(key, dims, pieces, -0.22, 0.18) if pieces else 1.0
    values = jax.random.normal(key, dims, jnp.float32) * deviation * factor_of
    return jnp.minimum(jnp.maximum(values, -most), most).astype(dtype)


def setup_inputs(seed: int = 0) -> dict:
    streams_of = jax.random.split(jax.random.key(seed), 8)
    return {
        "queries": draw_queries(jax.random.fold_in(streams_of[7], 71), 0),
        "resp_keys": centred(streams_of[1], (RROWS, RTOK, KVH * HD), 1.0, 6.0, ((0, 8), (1, 32))),
        "resp_values": centred(streams_of[2], (RROWS, RTOK, KVH * HD), 1.0, 6.0, ((0, 8), (1, 32))),
        "prompt_keys": draw_prompt_keys(jax.random.fold_in(streams_of[7], 71), 0),
        "prompt_values": centred(streams_of[4], (PROMPTS, PLEN, KVH * HD), 1.0, 6.0, ((1, 32),)),
        "response_prompt": draw_response_prompt(jax.random.fold_in(streams_of[7], 71), 0),
        "out_grad": centred(streams_of[6], (RROWS, RTOK, H * HD), 1.0, 6.0, ((0, 8), (1, 32))),
    }


def head_pass(query_head, key_head, value_head, grad_head, allowed, scaling):
    query_wide = query_head.astype(jnp.float32)
    key_wide = key_head.astype(jnp.float32)
    value_wide = value_head.astype(jnp.float32)
    grad_wide = grad_head.astype(jnp.float32)
    scores = jnp.einsum('qgd,kd->gqk', query_wide, key_wide) * scaling
    scores = jnp.where(allowed[None], scores, -jnp.inf)
    top_score = lax.optimization_barrier(jnp.max(scores, axis=2, keepdims=True))
    weights = jnp.exp(scores - top_score)
    probs = weights / lax.optimization_barrier(jnp.sum(weights, axis=2, keepdims=True))
    probs_low = lax.optimization_barrier(probs.astype(jnp.bfloat16)).astype(jnp.float32)
    attended = jnp.einsum('gqk,kd->qgd', probs_low, value_wide).astype(jnp.bfloat16)
    prob_grad = jnp.einsum('qgd,kd->gqk', grad_wide, value_wide)
    centre = lax.optimization_barrier(jnp.sum(probs * prob_grad, axis=2, keepdims=True))
    score_grad = lax.optimization_barrier((probs * (prob_grad - centre)).astype(jnp.bfloat16)).astype(jnp.float32)
    query_grad = (jnp.einsum('gqk,kd->qgd', score_grad, key_wide) * scaling).astype(jnp.bfloat16)
    key_grad = jnp.einsum('gqk,qgd->kd', score_grad, query_wide) * scaling
    value_grad = jnp.einsum('gqk,qgd->kd', probs_low, grad_wide)
    return (attended, query_grad, key_grad, value_grad)

def reference(queries, resp_keys, resp_values, prompt_keys, prompt_values, response_prompt, out_grad):
    scaling = 1.0 / math.sqrt(HD)
    group_size = H // KVH
    query_all = queries.reshape(RESPONSES, RLEN, KVH, group_size, HD)
    grad_all = out_grad.reshape(RESPONSES, RLEN, KVH, group_size, HD)
    rkey_all = resp_keys.reshape(RESPONSES, RLEN, KVH, HD)
    rval_all = resp_values.reshape(RESPONSES, RLEN, KVH, HD)
    pkey_all = prompt_keys.reshape(PROMPTS, PLEN, KVH, HD)
    pval_all = prompt_values.reshape(PROMPTS, PLEN, KVH, HD)
    positions = jnp.arange(RLEN)
    allowed = jnp.concatenate([jnp.ones((RLEN, PLEN), bool), positions[None, :] <= positions[:, None]], axis=1)

    def one_response(carry_grads, inputs_one):
        query_one, grad_one, rkey_one, rval_one, prompt_index = inputs_one
        key_full = jnp.concatenate([lax.dynamic_index_in_dim(pkey_all, prompt_index, 0, False), rkey_one], axis=0)
        value_full = jnp.concatenate([lax.dynamic_index_in_dim(pval_all, prompt_index, 0, False), rval_one], axis=0)

        def per_head(head_inputs):
            return head_pass(head_inputs[0], head_inputs[1], head_inputs[2], head_inputs[3], allowed, scaling)
        attended, query_grad, key_grad, value_grad = lax.map(per_head, (query_one.transpose(1, 0, 2, 3), key_full.transpose(1, 0, 2), value_full.transpose(1, 0, 2), grad_one.transpose(1, 0, 2, 3)))
        attended = attended.transpose(1, 0, 2, 3).reshape(RLEN, H * HD)
        query_grad = query_grad.transpose(1, 0, 2, 3).reshape(RLEN, H * HD)
        key_grad = key_grad.transpose(1, 0, 2)
        value_grad = value_grad.transpose(1, 0, 2)
        onehot = (jnp.arange(PROMPTS) == prompt_index).astype(jnp.float32)
        new_keys = carry_grads[0] + onehot[:, None, None, None] * key_grad[None, :PLEN]
        new_values = carry_grads[1] + onehot[:, None, None, None] * value_grad[None, :PLEN]
        resp_kg = key_grad[PLEN:].reshape(RLEN, KVH * HD).astype(jnp.bfloat16)
        resp_vg = value_grad[PLEN:].reshape(RLEN, KVH * HD).astype(jnp.bfloat16)
        return ((new_keys, new_values), (attended, query_grad, resp_kg, resp_vg))
    start_grads = (jnp.zeros((PROMPTS, PLEN, KVH, HD), jnp.float32), jnp.zeros((PROMPTS, PLEN, KVH, HD), jnp.float32))
    final_grads, outputs = lax.scan(one_response, start_grads, (query_all, grad_all, rkey_all, rval_all, response_prompt.astype(jnp.int32)))
    attended = outputs[0].reshape(RROWS, RTOK, H * HD)
    query_grad = outputs[1].reshape(RROWS, RTOK, H * HD)
    resp_key_grad = outputs[2].reshape(RROWS, RTOK, KVH * HD)
    resp_value_grad = outputs[3].reshape(RROWS, RTOK, KVH * HD)
    prompt_key_grad = final_grads[0].reshape(PROMPTS, PLEN, KVH * HD).astype(jnp.bfloat16)
    prompt_value_grad = final_grads[1].reshape(PROMPTS, PLEN, KVH * HD).astype(jnp.bfloat16)
    return (attended, query_grad, resp_key_grad, resp_value_grad, prompt_key_grad, prompt_value_grad)
```

```python
import math

import jax
import jax.numpy as jnp
from jax import lax
from jax.experimental import pallas as pl
from jax.experimental.pallas import tpu as pltpu
from jax.sharding import PartitionSpec as P

F32 = jnp.float32
BF16 = jnp.bfloat16
HD = 128
SPAN = 128
SCALING = 1.0 / math.sqrt(HD)
SCALING2 = SCALING * math.log2(math.e)
MESH = pl.DeviceIdType.MESH

NT = (((1,), (1,)), ((), ()))
NN = (((1,), (0,)), ((), ()))
TN = (((0,), (0,)), ((), ()))


def dot(a, b, dims):
    return lax.dot_general(a, b, dims, preferred_element_type=F32)


def head_pass(h, valid, qb, db, kv, gacc, ob, qgb, s_scr, d_scr):
    row = lax.broadcasted_iota(jnp.int32, (256, 256), 0)
    col = lax.broadcasted_iota(jnp.int32, (256, 256), 1)
    keep = row <= col
    for g in range(4):
        lanes = slice(g * HD, (g + 1) * HD)
        slot = g % 2
        qg = qb[h, :, :, lanes].reshape(256, HD)
        dog = db[h, :, :, lanes].reshape(256, HD)
        top = None
        for j in range(8):
            s = dot(kv[h, j, 0], qg, NT) * SCALING2
            if j == 4:
                s = jnp.where(keep, s, -jnp.inf)
            s_scr[slot, j] = s
            top_j = jnp.max(s, axis=0, keepdims=True)
            if j > 4:
                top_j = jnp.where(valid[j - 4], top_j, -jnp.inf)
            top = top_j if top is None else jnp.maximum(top, top_j)
        total = None
        centre = None
        for j in range(8):
            shift = top if j <= 4 else jnp.where(valid[j - 4], top, jnp.inf)
            w = jnp.exp2(s_scr[slot, j] - shift)
            dp = dot(kv[h, j, 1], dog, NT)
            s_scr[slot, j] = w
            d_scr[slot, j] = dp
            total_j = jnp.sum(w, axis=0, keepdims=True)
            centre_j = jnp.sum(w * dp, axis=0, keepdims=True)
            total = total_j if total is None else total + total_j
            centre = centre_j if centre is None else centre + centre_j
        inv = 1.0 / total
        centre = centre * inv
        out_t = None
        qgrad_t = None
        for j in range(8):
            probs = s_scr[slot, j] * inv
            score_grad = (probs * (d_scr[slot, j] - centre)).astype(BF16)
            probs_low = probs.astype(BF16)
            dv = dot(probs_low, dog, NN)
            dk = dot(score_grad, qg, NN)
            if g == 0:
                gacc[j, 1] = dv
                gacc[j, 0] = dk
            else:
                gacc[j, 1] += dv
                gacc[j, 0] += dk
            out_j = dot(kv[h, j, 1], probs_low, TN)
            qgrad_j = dot(kv[h, j, 0], score_grad, TN)
            out_t = out_j if out_t is None else out_t + out_j
            qgrad_t = qgrad_j if qgrad_t is None else qgrad_t + qgrad_j
        ob[h, :, :, lanes] = out_t.T.astype(BF16).reshape(2, SPAN, HD)
        qgb[h, :, :, lanes] = (qgrad_t * SCALING).T.astype(BF16).reshape(2, SPAN, HD)


def kernel(
    rp_ref, q_ref, do_ref, rk_ref, rv_ref, pk_ref, pv_ref,
    o_ref, qg_ref, rkg_ref, rvg_ref, pkg_ref, pvg_ref,
    qb, db, kv, relay, sel, gacc, st, sr, ob, qgb, ar, zs, zr, fo, gr, racc, s_scr, d_scr,
    r_z, r_p, r_kv, r_q, r_d, r_o, r_qg, r_g, r_a, r_zz, r_f,
    s_z, s_p, s_kv, s_q, s_d, s_o, s_qg, s_g, s_a, s_zz, s_f,
):
    seq = lax.axis_index("seq")
    resp = lax.axis_index("resp")
    x_lo = seq // 16
    z = (seq // 2) % 8
    core = seq % 2
    chip = z % 4
    z_hi = z // 4
    plane = resp * 2 + x_lo
    head_core = resp // 4
    own_half = core == head_core

    def seq_of(x, zz, k):
        return x * 16 + zz * 2 + k

    def device(s, r):
        return {"seq": s, "resp": r}

    def remote(src, dst, send, recv, s, r):
        return pltpu.make_async_remote_copy(
            src_ref=src, dst_ref=dst, send_sem=send, recv_sem=recv,
            device_id=device(s, r), device_id_type=MESH,
        )

    def wait_for(ref, sem):
        pltpu.make_async_copy(ref, ref, sem).wait()

    def cols(start, width):
        return pl.ds(pl.multiple_of(start, 128), width)

    barrier = pltpu.get_barrier_semaphore()

    def greet(s, r):
        pl.semaphore_signal(barrier, inc=1, device_id=device(s, r), device_id_type=MESH)

    place = resp * 4 + x_lo * 2 + core

    def greet_plane(t, _):
        other = (place + t) % 32
        greet(seq_of((other // 2) % 2, z, other % 2), other // 4)
        return 0

    lax.fori_loop(1, 32, greet_plane, 0)

    def greet_line(t, _):
        greet(seq_of(x_lo, (z + t) % 8, core), resp)
        return 0

    lax.fori_loop(1, 8, greet_line, 0)

    def greet_group(t, _):
        greet(seq_of(x_lo, z_hi * 4 + (chip + t) % 4, 1 - core), resp)
        return 0

    lax.fori_loop(1, 4, greet_group, 0)

    for d in range(1, 4):

        @pl.when(chip < d)
        def _():
            for h in range(4):
                kv[h, 4 + d] = jnp.zeros((2, 256, HD), BF16)

    pl.semaphore_wait(barrier, 41)

    mine = cols(resp * HD, HD)
    for which, src in enumerate((pk_ref, pv_ref)):
        pltpu.make_async_copy(src.at[:, :, mine], relay.at[which, :, z], r_z).start()

        def send_line(t, _, which=which, src=src):
            remote(
                src.at[:, :, mine], relay.at[which, :, z], s_z, r_z,
                seq_of(x_lo, (z + t) % 8, core), resp,
            ).start()
            return 0

        lax.fori_loop(1, 8, send_line, 0)

    def rotated(step):
        return (step + resp) % 4

    def send_inputs(step):
        h = rotated(step)
        own = cols((core * 4 + h) * 512, 512)
        other = cols(((1 - core) * 4 + h) * 512, 512)
        sibling = seq_of(x_lo, z, 1 - core)
        for src, dst, send, recv in ((q_ref, qb, s_q, r_q), (do_ref, db, s_d, r_d)):
            remote(src.at[:, other], dst.at[h, core], send, recv.at[h], sibling, resp).start()
            pltpu.make_async_copy(src.at[:, own], dst.at[h, core], recv.at[h]).start()
        rows = pl.ds(pl.multiple_of(core * SPAN, SPAN), SPAN)
        for which, src in enumerate((rk_ref, rv_ref)):
            own = cols((core * 4 + h) * HD, HD)
            other = cols(((1 - core) * 4 + h) * HD, HD)
            dst = kv.at[h, 4, which, rows]
            pltpu.make_async_copy(src.at[:, own], dst, r_kv.at[h, 0]).start()
            remote(src.at[:, other], dst, s_kv.at[0], r_kv.at[h, 0], sibling, resp).start()
        for d in range(1, 4):

            @pl.when(chip + d <= 3)
            def _():
                for k in range(2):
                    for which, src in enumerate((rk_ref, rv_ref)):
                        remote(
                            src.at[:, cols((k * 4 + h) * HD, HD)],
                            kv.at[h, 4 + d, which, rows],
                            s_kv.at[d], r_kv.at[h, d],
                            seq_of(x_lo, z + d, k), resp,
                        ).start()

    send_inputs(0)

    wait_for(relay, r_z)
    quarter = x_lo * 2 + core

    def send_plane(step, _):
        for hi in range(2):
            for xl in range(2):
                r = (resp + 4 - step) % 4 + 4 * ((resp // 4 + hi) % 2)
                x = (x_lo + xl) % 2
                second = rp_ref[r * 4 + x * 2 + z_hi] == 1
                at = step * 4 + hi * 2 + xl
                for which in range(2):
                    sel[at, which] = jnp.where(
                        second, relay[which, 1].reshape(256, HD), relay[which, 0].reshape(256, HD)
                    )
                dst = kv.at[resp % 4, quarter]
                recv = r_p.at[resp % 4]
                here = (at == 0) & own_half

                @pl.when(here)
                def _():
                    pltpu.make_async_copy(sel.at[at], dst, recv).start()

                @pl.when(jnp.logical_not(here))
                def _():
                    remote(
                        sel.at[at], dst, s_p.at[at], recv, seq_of(x, z, head_core), r
                    ).start()

        return 0

    lax.fori_loop(0, 4, send_plane, 0)
    for step in range(1, 4):
        send_inputs(step)

    valid = [chip >= d for d in range(4)]

    def run_head(step, _):
        h = rotated(step)
        wait_for(qb.at[h], r_q.at[h])
        wait_for(db.at[h], r_d.at[h])
        for d in range(4):

            @pl.when(chip >= d)
            def _():
                wait_for(kv.at[h, 4 + d], r_kv.at[h, d])

        wait_for(kv.at[h, pl.ds(0, 4)], r_p.at[h])
        head_pass(h, valid, qb, db, kv, gacc, ob, qgb, s_scr, d_scr)
        for j in range(4):
            st[h, j, 0] = (gacc[j, 0] * SCALING).astype(BF16)
            st[h, j, 1] = gacc[j, 1].astype(BF16)
        head = core * 4 + h
        for x in range(2):
            for k in range(2):
                here = (head == resp) & (x == x_lo) & (k == core)
                src = st.at[h, x * 2 + k]

                @pl.when(here)
                def _():
                    pltpu.make_async_copy(src, ar.at[plane], r_a).start()

                @pl.when(jnp.logical_not(here))
                def _():
                    remote(
                        src, ar.at[plane], s_a.at[h, x * 2 + k], r_a, seq_of(x, z, k), head
                    ).start()

        for d in range(4):

            @pl.when(chip >= d)
            def _():
                for k in range(2):
                    rows = slice(k * SPAN, (k + 1) * SPAN)
                    sr[h, d, k, 0] = (gacc[4 + d, 0, rows] * SCALING).astype(BF16)
                    sr[h, d, k, 1] = gacc[4 + d, 1, rows].astype(BF16)
                if d == 0:
                    dst = gr.at[0, head]
                    pltpu.make_async_copy(sr.at[h, 0, core], dst, r_g.at[0]).start()
                    remote(
                        sr.at[h, 0, 1 - core], dst, s_g.at[0], r_g.at[0],
                        seq_of(x_lo, z, 1 - core), resp,
                    ).start()
                else:
                    for k in range(2):
                        remote(
                            sr.at[h, d, k], gr.at[d, head], s_g.at[d], r_g.at[d],
                            seq_of(x_lo, z - d, k), resp,
                        ).start()

        where = cols(head * 512, 512)
        for src, dst, send, recv in ((ob, o_ref, s_o, r_o), (qgb, qg_ref, s_qg, r_qg)):
            pltpu.make_async_copy(src.at[h, core], dst.at[:, where], recv).start()
            remote(
                src.at[h, 1 - core], dst.at[:, where], send, recv,
                seq_of(x_lo, z, 1 - core), resp,
            ).start()
        return 0

    lax.fori_loop(0, 4, run_head, 0)

    wait_for(ar, r_a)
    second = [rp_ref[(a // 2) * 4 + (a % 2) * 2 + z_hi] == 1 for a in range(16)]

    def sum_plane(t, _):
        to = (z + t) % 8
        rows = pl.ds(pl.multiple_of(to * 32, 32), 32)
        for which in range(2):
            sums = [jnp.zeros((32, HD), F32), jnp.zeros((32, HD), F32)]
            for a in range(16):
                term = ar[a, which, rows].astype(F32)
                sums[0] += jnp.where(second[a], 0.0, term)
                sums[1] += jnp.where(second[a], term, 0.0)
            for p in range(2):
                zs[to, p, which] = sums[p].astype(BF16)

        @pl.when(t == 0)
        def _():
            pltpu.make_async_copy(zs.at[to], zr.at[z], r_zz).start()

        @pl.when(t > 0)
        def _():
            remote(
                zs.at[to], zr.at[z], s_zz, r_zz, seq_of(x_lo, to, core), resp
            ).start()

        return 0

    lax.fori_loop(0, 8, sum_plane, 0)

    wait_for(gr.at[0], r_g.at[0])
    racc[...] = gr[0].astype(F32)
    for d in range(1, 4):

        @pl.when(chip + d <= 3)
        def _():
            wait_for(gr.at[d], r_g.at[d])
            racc[...] += gr[d].astype(F32)

    for n in range(8):
        rkg_ref[:, n * HD : (n + 1) * HD] = racc[n, 0].astype(BF16)
        rvg_ref[:, n * HD : (n + 1) * HD] = racc[n, 1].astype(BF16)

    wait_for(zr, r_zz)
    for which in range(2):
        for p in range(2):
            final = zr[0, p, which].astype(F32)
            for n in range(1, 8):
                final = final + zr[n, p, which].astype(F32)
            fo[which, p] = final.astype(BF16)
    for which, dst in enumerate((pkg_ref, pvg_ref)):
        pltpu.make_async_copy(fo.at[which], dst.at[:, :, mine], r_f.at[which]).start()

        def send_replica(t, _, which=which, dst=dst):
            remote(
                fo.at[which], dst.at[:, :, mine], s_f.at[which], r_f.at[which],
                seq, (resp + t) % 8,
            ).start()
            return 0

        lax.fori_loop(1, 8, send_replica, 0)

    wait_for(o_ref, r_o)
    wait_for(qg_ref, r_qg)
    wait_for(pkg_ref, r_f.at[0])
    wait_for(pvg_ref, r_f.at[1])

    wait_for(relay.at[:, :, pl.ds(0, 7)], s_z)
    for at in range(16):
        if at == 0:

            @pl.when(jnp.logical_not(own_half))
            def _():
                wait_for(sel.at[0], s_p.at[0])
        else:
            wait_for(sel.at[at], s_p.at[at])
    wait_for(kv.at[0, pl.ds(0, 2)], s_kv.at[0])
    wait_for(gr.at[0, pl.ds(0, 4)], s_g.at[0])
    for d in range(1, 4):

        @pl.when(chip + d <= 3)
        def _():
            wait_for(kv.at[0, pl.ds(0, 4)], s_kv.at[d])

        @pl.when(chip >= d)
        def _():
            wait_for(gr.at[0], s_g.at[d])

    wait_for(qb.at[:, 0], s_q)
    wait_for(db.at[:, 0], s_d)
    wait_for(ob.at[:, 0], s_o)
    wait_for(qgb.at[:, 0], s_qg)
    for h in range(4):
        for n in range(4):
            here = (core * 4 + h == resp) & (n == quarter)

            @pl.when(jnp.logical_not(here))
            def _():
                wait_for(st.at[h, n], s_a.at[h, n])

    wait_for(zr.at[pl.ds(0, 7)], s_zz)
    for which in range(2):
        wait_for(zr.at[pl.ds(0, 7), 0], s_f.at[which])


def body(queries, resp_keys, resp_values, prompt_keys, prompt_values, response_prompt, out_grad):
    anywhere = pl.BlockSpec(memory_space=pl.ANY)
    vmem = pl.BlockSpec(memory_space=pltpu.VMEM)
    dma = pltpu.SemaphoreType.DMA
    rows = jax.ShapeDtypeStruct((SPAN, 4096), BF16)
    block = jax.ShapeDtypeStruct((SPAN, 1024), BF16)
    shard = jax.ShapeDtypeStruct((2, 32, 1024), BF16)
    attended, query_grad, rkg, rvg, pkg, pvg = pl.pallas_call(
        kernel,
        out_shape=(rows, rows, block, block, shard, shard),
        in_specs=[pl.BlockSpec(memory_space=pltpu.SMEM)] + [anywhere] * 6,
        out_specs=(anywhere, anywhere, vmem, vmem, anywhere, anywhere),
        scratch_shapes=[
            pltpu.VMEM((4, 2, SPAN, 512), BF16),
            pltpu.VMEM((4, 2, SPAN, 512), BF16),
            pltpu.VMEM((4, 8, 2, 256, HD), BF16),
            pltpu.VMEM((2, 2, 8, 32, HD), BF16),
            pltpu.VMEM((16, 2, 256, HD), BF16),
            pltpu.VMEM((8, 2, 256, HD), F32),
            pltpu.VMEM((4, 4, 2, 256, HD), BF16),
            pltpu.VMEM((4, 4, 2, 2, SPAN, HD), BF16),
            pltpu.VMEM((4, 2, SPAN, 512), BF16),
            pltpu.VMEM((4, 2, SPAN, 512), BF16),
            pltpu.VMEM((16, 2, 256, HD), BF16),
            pltpu.VMEM((8, 2, 2, 32, HD), BF16),
            pltpu.VMEM((8, 2, 2, 32, HD), BF16),
            pltpu.VMEM((2, 2, 32, HD), BF16),
            pltpu.VMEM((4, 8, 2, SPAN, HD), BF16),
            pltpu.VMEM((8, 2, SPAN, HD), F32),
            pltpu.VMEM((2, 8, 256, 256), F32),
            pltpu.VMEM((2, 8, 256, 256), F32),
            dma(()),
            dma((4,)),
            dma((4, 4)),
            dma((4,)),
            dma((4,)),
            dma(()),
            dma(()),
            dma((4,)),
            dma(()),
            dma(()),
            dma((2,)),
            dma(()),
            dma((16,)),
            dma((4,)),
            dma(()),
            dma(()),
            dma(()),
            dma(()),
            dma((4,)),
            dma((4, 4)),
            dma(()),
            dma((2,)),
        ],
        compiler_params=pltpu.CompilerParams(
            collective_id=0, has_side_effects=True, vmem_limit_bytes=56 * 1024 * 1024
        ),
        name="attention_step",
    )(
        response_prompt, queries[0], out_grad[0], resp_keys[0], resp_values[0],
        prompt_keys, prompt_values,
    )
    return (attended[None], query_grad[None], rkg[None], rvg[None], pkg, pvg)


def solution(mesh):
    by_row = P("resp", "seq", None)
    shared = P(None, "seq", None)
    return jax.shard_map(
        body,
        mesh=mesh,
        in_specs=(by_row, by_row, by_row, shared, shared, P(), by_row),
        out_specs=(by_row, by_row, by_row, by_row, shared, shared),
        check_vma=False,
    )
```

```python
import math

import jax
import jax.numpy as jnp
from jax import lax
from jax.experimental import pallas as pl
from jax.experimental.pallas import tpu as pltpu
from jax.sharding import PartitionSpec as P

F32 = jnp.float32
BF16 = jnp.bfloat16
HD = 128
SPAN = 128
SCALING = 1.0 / math.sqrt(HD)
SCALING2 = SCALING * math.log2(math.e)
MESH = pl.DeviceIdType.MESH

NT = (((1,), (1,)), ((), ()))
NN = (((1,), (0,)), ((), ()))
TN = (((0,), (0,)), ((), ()))


def dot(a, b, dims):
    return lax.dot_general(a, b, dims, preferred_element_type=F32)


def head_pass(h, valid, between, qb, db, kv, gacc, ob, qgb, s_scr, d_scr):
    row = lax.broadcasted_iota(jnp.int32, (256, 256), 0)
    col = lax.broadcasted_iota(jnp.int32, (256, 256), 1)
    keep = row <= col
    for g in range(4):
        lanes = slice(g * HD, (g + 1) * HD)
        slot = g % 2
        qg = qb[h, :, :, lanes].reshape(256, HD)
        dog = db[h, :, :, lanes].reshape(256, HD)
        top = None
        for j in range(8):
            s = dot(kv[h, j, 0], qg, NT) * SCALING2
            if j == 4:
                s = jnp.where(keep, s, -jnp.inf)
            s_scr[slot, j] = s
            top_j = jnp.max(s, axis=0, keepdims=True)
            if j > 4:
                top_j = jnp.where(valid[j - 4], top_j, -jnp.inf)
            top = top_j if top is None else jnp.maximum(top, top_j)
        total = None
        centre = None
        for j in range(8):
            shift = top if j <= 4 else jnp.where(valid[j - 4], top, jnp.inf)
            w = jnp.exp2(s_scr[slot, j] - shift)
            dp = dot(kv[h, j, 1], dog, NT)
            s_scr[slot, j] = w
            d_scr[slot, j] = dp
            total_j = jnp.sum(w, axis=0, keepdims=True)
            centre_j = jnp.sum(w * dp, axis=0, keepdims=True)
            total = total_j if total is None else total + total_j
            centre = centre_j if centre is None else centre + centre_j
        inv = 1.0 / total
        centre = centre * inv
        out_t = None
        qgrad_t = None
        for j in range(8):
            probs = s_scr[slot, j] * inv
            score_grad = (probs * (d_scr[slot, j] - centre)).astype(BF16)
            probs_low = probs.astype(BF16)
            dv = dot(probs_low, dog, NN)
            dk = dot(score_grad, qg, NN)
            if g == 0:
                gacc[j, 1] = dv
                gacc[j, 0] = dk
            else:
                gacc[j, 1] += dv
                gacc[j, 0] += dk
            out_j = dot(kv[h, j, 1], probs_low, TN)
            qgrad_j = dot(kv[h, j, 0], score_grad, TN)
            out_t = out_j if out_t is None else out_t + out_j
            qgrad_t = qgrad_j if qgrad_t is None else qgrad_t + qgrad_j
        ob[h, :, :, lanes] = out_t.T.astype(BF16).reshape(2, SPAN, HD)
        qgb[h, :, :, lanes] = (qgrad_t * SCALING).T.astype(BF16).reshape(2, SPAN, HD)
        between(g)


def kernel(
    rp_ref, q_ref, do_ref, rk_ref, rv_ref, pk_ref, pv_ref,
    o_ref, qg_ref, rkg_ref, rvg_ref, pkg_ref, pvg_ref,
    qb, db, kv, stage, relay, sel, gacc, st, sr, ob, qgb, ar, zs, zr, fo, fr, gr, mb, racc, s_scr, d_scr,
    r_s, r_z, r_p, r_kv, r_q, r_d, r_o, r_qg, r_g, r_m, r_a, r_zz, r_f,
    s_z, s_p, s_kv, s_w, s_q, s_d, s_o, s_qg, s_g, s_a, s_zz, s_f,
):
    seq = lax.axis_index("seq")
    resp = lax.axis_index("resp")
    x_lo = seq // 16
    z = (seq // 2) % 8
    core = seq % 2
    chip = z % 4
    z_hi = z // 4
    plane = resp * 2 + x_lo
    head_core = resp // 4
    own_half = core == head_core

    def seq_of(x, zz, k):
        return x * 16 + zz * 2 + k

    def device(s, r):
        return {"seq": s, "resp": r}

    def remote(src, dst, send, recv, s, r):
        return pltpu.make_async_remote_copy(
            src_ref=src, dst_ref=dst, send_sem=send, recv_sem=recv,
            device_id=device(s, r), device_id_type=MESH,
        )

    def wait_for(ref, sem):
        pltpu.make_async_copy(ref, ref, sem).wait()

    def cols(start, width):
        return pl.ds(pl.multiple_of(start, 128), width)

    mine = cols(resp * HD, HD)
    for which, src in enumerate((pk_ref, pv_ref)):
        pltpu.make_async_copy(src.at[:, :, mine], stage.at[which], r_s).start()

    barrier = pltpu.get_barrier_semaphore()

    def greet(s, r):
        pl.semaphore_signal(barrier, inc=1, device_id=device(s, r), device_id_type=MESH)

    place = resp * 4 + x_lo * 2 + core

    def greet_plane(t, _):
        other = (place + t) % 32
        greet(seq_of((other // 2) % 2, z, other % 2), other // 4)
        return 0

    lax.fori_loop(1, 32, greet_plane, 0)

    def greet_line(t, _):
        greet(seq_of(x_lo, (z + t) % 8, core), resp)
        return 0

    lax.fori_loop(1, 8, greet_line, 0)

    def greet_group(t, _):
        greet(seq_of(x_lo, z_hi * 4 + (chip + t) % 4, 1 - core), resp)
        return 0

    lax.fori_loop(1, 4, greet_group, 0)

    for d in range(1, 4):

        @pl.when(chip < d)
        def _():
            for h in range(4):
                kv[h, 4 + d] = jnp.zeros((2, 256, HD), BF16)

    pl.semaphore_wait(barrier, 41)

    wait_for(stage, r_s)
    pltpu.make_async_copy(stage, relay.at[z], r_z).start()

    def send_line(t, _):
        remote(stage, relay.at[z], s_z, r_z, seq_of(x_lo, (z + t) % 8, core), resp).start()
        return 0

    lax.fori_loop(1, 8, send_line, 0)

    y = resp // 2
    x_hi = resp % 2

    def head_at(step, k):
        odd = (y + step // 2) % 2
        away = ((y - 2 * k - odd + 4) % 4) // 2
        return odd * 2 + (x_hi + step + away) % 2

    def send_inputs(step):
        h = head_at(step, core)
        h_other = head_at(step, 1 - core)
        own = cols((core * 4 + h) * 512, 512)
        other = cols(((1 - core) * 4 + h_other) * 512, 512)
        sibling = seq_of(x_lo, z, 1 - core)
        for src, dst, send, recv in ((q_ref, qb, s_q, r_q), (do_ref, db, s_d, r_d)):
            remote(
                src.at[:, other], dst.at[h_other, core], send, recv.at[h_other], sibling, resp
            ).start()
            pltpu.make_async_copy(src.at[:, own], dst.at[h, core], recv.at[h]).start()
        rows = pl.ds(pl.multiple_of(core * SPAN, SPAN), SPAN)
        for which, src in enumerate((rk_ref, rv_ref)):
            own = cols((core * 4 + h) * HD, HD)
            other = cols(((1 - core) * 4 + h_other) * HD, HD)
            pltpu.make_async_copy(
                src.at[:, own], kv.at[h, 4, which, rows], r_kv.at[h, 0]
            ).start()
            remote(
                src.at[:, other], kv.at[h_other, 4, which, rows],
                s_kv.at[0], r_kv.at[h_other, 0], sibling, resp,
            ).start()
        send_keys(step, 1)

    def sends_to(d):
        return (chip + d <= 3) if d != 2 else (chip == 0)

    def send_keys(step, d):
        rows = pl.ds(pl.multiple_of(core * SPAN, SPAN), SPAN)

        @pl.when(sends_to(d))
        def _():
            for k in range(2):
                to = head_at(step, k)
                for which, src in enumerate((rk_ref, rv_ref)):
                    remote(
                        src.at[:, cols((k * 4 + to) * HD, HD)],
                        kv.at[to, 4 + d, which, rows],
                        s_kv.at[d], r_kv.at[to, d],
                        seq_of(x_lo, z + d, k), resp,
                    ).start()

    def hand_on(step):
        h = head_at(step, core)

        @pl.when(chip == 2)
        def _():
            wait_for(kv.at[h, 5], r_kv.at[h, 1])
            remote(
                kv.at[h, 5], kv.at[h, 6], s_w, r_kv.at[h, 2], seq_of(x_lo, z + 1, core), resp
            ).start()

    def merge(step):
        h = head_at(step, core)

        @pl.when(chip == 2)
        def _():
            wait_for(mb.at[h], r_m.at[h])
            sr[h, 1] = (sr[h, 1].astype(F32) + mb[h].astype(F32)).astype(BF16)
            for k in range(2):
                remote(
                    sr.at[h, 1, k], gr.at[1, core * 4 + h], s_g.at[1], r_g.at[1],
                    seq_of(x_lo, z - 1, k), resp,
                ).start()

    send_inputs(0)

    wait_for(relay, r_z)
    quarter = x_lo * 2 + core

    def send_plane(step):
        shift = 2 * (step % 2) + step // 2
        for hi in range(2):
            for xl in range(2):
                r = ((y + shift + 2 * hi) % 4) * 2 + (x_hi + hi) % 2
                x = (x_lo + xl) % 2
                second = rp_ref[r * 4 + x * 2 + z_hi] == 1
                at = step * 4 + hi * 2 + xl
                for which in range(2):
                    sel[at, which] = jnp.where(
                        second,
                        relay[:, which, 1].reshape(256, HD),
                        relay[:, which, 0].reshape(256, HD),
                    )
                dst = kv.at[resp % 4, quarter]
                recv = r_p.at[resp % 4]
                here = (at == 0) & own_half

                @pl.when(here)
                def _():
                    pltpu.make_async_copy(sel.at[at], dst, recv).start()

                @pl.when(jnp.logical_not(here))
                def _():
                    remote(
                        sel.at[at], dst, s_p.at[at], recv, seq_of(x, z, head_core), r
                    ).start()

    send_plane(0)
    send_keys(0, 2)
    send_keys(0, 3)
    hand_on(0)

    valid = [chip >= d for d in range(4)]

    def run_head(step, _):
        h = head_at(step, core)
        wait_for(qb.at[h], r_q.at[h])
        wait_for(db.at[h], r_d.at[h])
        for d in range(4):

            @pl.when((chip >= d) if d != 1 else (chip % 2 == 1))
            def _():
                wait_for(kv.at[h, 4 + d], r_kv.at[h, d])

        wait_for(kv.at[h, pl.ds(0, 4)], r_p.at[h])

        @pl.when(step == 0)
        def _():
            send_plane(1)
            send_inputs(1)

        def between(g):
            if g == 0:

                @pl.when(step == 0)
                def _():
                    send_keys(1, 2)
                    send_keys(1, 3)
            elif g == 1:

                @pl.when(step < 3)
                def _():
                    hand_on(step + 1)
            elif g == 2:

                @pl.when(step < 2)
                def _():
                    send_plane(step + 2)
                    send_inputs(step + 2)
                    send_keys(step + 2, 2)
                    send_keys(step + 2, 3)

                @pl.when(step > 0)
                def _():
                    merge(step - 1)

        head_pass(h, valid, between, qb, db, kv, gacc, ob, qgb, s_scr, d_scr)
        for j in range(4):
            st[h, j, 0] = (gacc[j, 0] * SCALING).astype(BF16)
            st[h, j, 1] = gacc[j, 1].astype(BF16)
        head = core * 4 + h
        for x in range(2):
            for k in range(2):
                here = (head == resp) & (x == x_lo) & (k == core)
                src = st.at[h, x * 2 + k]

                @pl.when(here)
                def _():
                    pltpu.make_async_copy(src, ar.at[plane], r_a).start()

                @pl.when(jnp.logical_not(here))
                def _():
                    remote(
                        src, ar.at[plane], s_a.at[h, x * 2 + k], r_a, seq_of(x, z, k), head
                    ).start()

        def send_terms(d):
            for k in range(2):
                remote(
                    sr.at[h, d, k], gr.at[d, head], s_g.at[d], r_g.at[d],
                    seq_of(x_lo, z - d, k), resp,
                ).start()

        for d in range(4):

            @pl.when(chip >= d)
            def _():
                for k in range(2):
                    rows = slice(k * SPAN, (k + 1) * SPAN)
                    sr[h, d, k, 0] = (gacc[4 + d, 0, rows] * SCALING).astype(BF16)
                    sr[h, d, k, 1] = gacc[4 + d, 1, rows].astype(BF16)
                if d == 0:
                    dst = gr.at[0, head]
                    pltpu.make_async_copy(sr.at[h, 0, core], dst, r_g.at[0]).start()
                    remote(
                        sr.at[h, 0, 1 - core], dst, s_g.at[0], r_g.at[0],
                        seq_of(x_lo, z, 1 - core), resp,
                    ).start()
                elif d == 1:

                    @pl.when(chip != 2)
                    def _():
                        send_terms(d)
                elif d == 2:

                    @pl.when(chip == 2)
                    def _():
                        send_terms(d)

                    @pl.when(chip == 3)
                    def _():
                        remote(
                            sr.at[h, 2], mb.at[h], s_g.at[2], r_m.at[h],
                            seq_of(x_lo, z - 1, core), resp,
                        ).start()
                else:
                    send_terms(d)

        where = cols(head * 512, 512)
        for src, dst, send, recv in ((ob, o_ref, s_o, r_o), (qgb, qg_ref, s_qg, r_qg)):
            pltpu.make_async_copy(src.at[h, core], dst.at[:, where], recv).start()
            remote(
                src.at[h, 1 - core], dst.at[:, where], send, recv,
                seq_of(x_lo, z, 1 - core), resp,
            ).start()
        return 0

    lax.fori_loop(0, 4, run_head, 0)

    merge(3)

    wait_for(ar, r_a)
    second = [rp_ref[(a // 2) * 4 + (a % 2) * 2 + z_hi] == 1 for a in range(16)]

    def sum_plane(t, _):
        to = (z + t) % 8
        rows = pl.ds(pl.multiple_of(to * 32, 32), 32)
        for which in range(2):
            sums = [jnp.zeros((32, HD), F32), jnp.zeros((32, HD), F32)]
            for a in range(16):
                term = ar[a, which, rows].astype(F32)
                sums[0] += jnp.where(second[a], 0.0, term)
                sums[1] += jnp.where(second[a], term, 0.0)
            for p in range(2):
                zs[to, p, which] = sums[p].astype(BF16)

        @pl.when(t == 0)
        def _():
            pltpu.make_async_copy(zs.at[to], zr.at[z], r_zz).start()

        @pl.when(t > 0)
        def _():
            remote(
                zs.at[to], zr.at[z], s_zz, r_zz, seq_of(x_lo, to, core), resp
            ).start()

        return 0

    lax.fori_loop(0, 8, sum_plane, 0)

    wait_for(gr.at[0], r_g.at[0])
    racc[...] = gr[0].astype(F32)
    for d in range(1, 4):

        @pl.when(sends_to(d))
        def _():
            wait_for(gr.at[d], r_g.at[d])
            racc[...] += gr[d].astype(F32)

    for n in range(8):
        rkg_ref[:, n * HD : (n + 1) * HD] = racc[n, 0].astype(BF16)
        rvg_ref[:, n * HD : (n + 1) * HD] = racc[n, 1].astype(BF16)

    wait_for(zr, r_zz)
    for which in range(2):
        for p in range(2):
            final = zr[0, p, which].astype(F32)
            for n in range(1, 8):
                final = final + zr[n, p, which].astype(F32)
            fo[which, p] = final.astype(BF16)
    pltpu.make_async_copy(fo, fr.at[resp], r_f).start()

    def send_replica(t, _):
        remote(fo, fr.at[resp], s_f, r_f, seq, (resp + t) % 8).start()
        return 0

    lax.fori_loop(1, 8, send_replica, 0)

    wait_for(o_ref, r_o)
    wait_for(qg_ref, r_qg)
    wait_for(fr, r_f)
    for n in range(8):
        pkg_ref[:, :, n * HD : (n + 1) * HD] = fr[n, 0]
        pvg_ref[:, :, n * HD : (n + 1) * HD] = fr[n, 1]

    wait_for(relay.at[pl.ds(0, 7)], s_z)
    for at in range(16):
        if at == 0:

            @pl.when(jnp.logical_not(own_half))
            def _():
                wait_for(sel.at[0], s_p.at[0])
        else:
            wait_for(sel.at[at], s_p.at[at])
    wait_for(kv.at[0, pl.ds(0, 2)], s_kv.at[0])
    wait_for(gr.at[0, pl.ds(0, 4)], s_g.at[0])
    for d in range(1, 4):

        @pl.when(sends_to(d))
        def _():
            wait_for(kv.at[0, pl.ds(0, 4)], s_kv.at[d])

        @pl.when(chip >= d)
        def _():
            wait_for(gr.at[0], s_g.at[d])

    @pl.when(chip == 2)
    def _():
        wait_for(kv.at[0, pl.ds(0, 4)], s_w)

    wait_for(qb.at[:, 0], s_q)
    wait_for(db.at[:, 0], s_d)
    wait_for(ob.at[:, 0], s_o)
    wait_for(qgb.at[:, 0], s_qg)
    for h in range(4):
        for n in range(4):
            here = (core * 4 + h == resp) & (n == quarter)

            @pl.when(jnp.logical_not(here))
            def _():
                wait_for(st.at[h, n], s_a.at[h, n])

    wait_for(zr.at[pl.ds(0, 7)], s_zz)
    wait_for(fr.at[pl.ds(0, 7)], s_f)


def finish(*refs):
    for src, dst in zip(refs[:6], refs[6:]):
        dst[...] = src[...]


def body(queries, resp_keys, resp_values, prompt_keys, prompt_values, response_prompt, out_grad):
    anywhere = pl.BlockSpec(memory_space=pl.ANY)
    vmem = pl.BlockSpec(memory_space=pltpu.VMEM)
    dma = pltpu.SemaphoreType.DMA
    rows = jax.ShapeDtypeStruct((SPAN, 4096), BF16)
    block = jax.ShapeDtypeStruct((SPAN, 1024), BF16)
    shard = jax.ShapeDtypeStruct((2, 32, 1024), BF16)
    results = pl.pallas_call(
        kernel,
        out_shape=(rows, rows, block, block, shard, shard),
        in_specs=[pl.BlockSpec(memory_space=pltpu.SMEM)] + [anywhere] * 6,
        out_specs=(anywhere, anywhere, vmem, vmem, vmem, vmem),
        scratch_shapes=[
            pltpu.VMEM((4, 2, SPAN, 512), BF16),
            pltpu.VMEM((4, 2, SPAN, 512), BF16),
            pltpu.VMEM((4, 8, 2, 256, HD), BF16),
            pltpu.VMEM((2, 2, 32, HD), BF16),
            pltpu.VMEM((8, 2, 2, 32, HD), BF16),
            pltpu.VMEM((16, 2, 256, HD), BF16),
            pltpu.VMEM((8, 2, 256, HD), F32),
            pltpu.VMEM((4, 4, 2, 256, HD), BF16),
            pltpu.VMEM((4, 4, 2, 2, SPAN, HD), BF16),
            pltpu.VMEM((4, 2, SPAN, 512), BF16),
            pltpu.VMEM((4, 2, SPAN, 512), BF16),
            pltpu.VMEM((16, 2, 256, HD), BF16),
            pltpu.VMEM((8, 2, 2, 32, HD), BF16),
            pltpu.VMEM((8, 2, 2, 32, HD), BF16),
            pltpu.VMEM((2, 2, 32, HD), BF16),
            pltpu.VMEM((8, 2, 2, 32, HD), BF16),
            pltpu.VMEM((4, 8, 2, SPAN, HD), BF16),
            pltpu.VMEM((4, 2, 2, SPAN, HD), BF16),
            pltpu.VMEM((8, 2, SPAN, HD), F32),
            pltpu.VMEM((2, 8, 256, 256), F32),
            pltpu.VMEM((2, 8, 256, 256), F32),
            dma(()),
            dma(()),
            dma((4,)),
            dma((4, 4)),
            dma((4,)),
            dma((4,)),
            dma(()),
            dma(()),
            dma((4,)),
            dma((4,)),
            dma(()),
            dma(()),
            dma(()),
            dma(()),
            dma((16,)),
            dma((4,)),
            dma(()),
            dma(()),
            dma(()),
            dma(()),
            dma(()),
            dma((4,)),
            dma((4, 4)),
            dma(()),
            dma(()),
        ],
        compiler_params=pltpu.CompilerParams(
            collective_id=0, has_side_effects=True, vmem_limit_bytes=56 * 1024 * 1024
        ),
        name="attention_step",
    )(
        response_prompt, queries[0], out_grad[0], resp_keys[0], resp_values[0],
        prompt_keys, prompt_values,
    )
    parts = (
        [pl.BlockSpec((SPAN, 1024), lambda i: (0, i))] * 2
        + [pl.BlockSpec((SPAN, 256), lambda i: (0, i))] * 2
        + [pl.BlockSpec((2, 32, 256), lambda i: (0, 0, i))] * 2
    )
    attended, query_grad, rkg, rvg, pkg, pvg = pl.pallas_call(
        finish,
        out_shape=(rows, rows, block, block, shard, shard),
        grid=(4,),
        in_specs=parts,
        out_specs=parts,
        name="finish",
    )(*results)
    return (attended[None], query_grad[None], rkg[None], rvg[None], pkg, pvg)


def solution(mesh):
    by_row = P("resp", "seq", None)
    shared = P(None, "seq", None)
    return jax.shard_map(
        body,
        mesh=mesh,
        in_specs=(by_row, by_row, by_row, shared, shared, P(), by_row),
        out_specs=(by_row, by_row, by_row, by_row, shared, shared),
        check_vma=False,
    )
```

```python
import math

import jax
import jax.numpy as jnp
from jax import lax
from jax.experimental import pallas as pl
from jax.experimental.pallas import tpu as pltpu
from jax.sharding import PartitionSpec as P

F32 = jnp.float32
BF16 = jnp.bfloat16
HD = 128
SPAN = 128
PART = 128
SCALING = 1.0 / math.sqrt(HD)
SCALING2 = SCALING * math.log2(math.e)
MESH = pl.DeviceIdType.MESH

NT = (((1,), (1,)), ((), ()))
NN = (((1,), (0,)), ((), ()))
TN = (((0,), (0,)), ((), ()))


def dot(a, b, dims):
    return lax.dot_general(a, b, dims, preferred_element_type=F32)


def head_pass(h, valid, between, qb, db, kv, gacc, ob, qgb, s_scr, d_scr):
    row = lax.broadcasted_iota(jnp.int32, (PART, 256), 0)
    col = lax.broadcasted_iota(jnp.int32, (PART, 256), 1)
    for g in range(4):
        lanes = slice(g * HD, (g + 1) * HD)
        slot = g % 2
        qg = qb[h, :, :, lanes].reshape(256, HD)
        dog = db[h, :, :, lanes].reshape(256, HD)
        tops, totals, centres = [], [], []
        for j in range(8):
            for at in range(0, 256, PART):
                part = slice(at, at + PART)
                s = dot(kv[h, j, 0, part], qg, NT) * SCALING2
                if j == 4:
                    s = jnp.where(row + at <= col, s, -jnp.inf)
                top = jnp.max(s, axis=0, keepdims=True)
                if j == 4:
                    top = jnp.maximum(top, -1e30)
                w = jnp.exp2(s - top)
                dp = dot(kv[h, j, 1, part], dog, NT)
                s_scr[slot, j, part] = w
                d_scr[slot, j, part] = dp
                tops.append(top if j <= 4 else jnp.where(valid[j - 4], top, -jnp.inf))
                totals.append(jnp.sum(w, axis=0, keepdims=True))
                centres.append(jnp.sum(w * dp, axis=0, keepdims=True))
        row_top = tops[0]
        for top in tops[1:]:
            row_top = jnp.maximum(row_top, top)
        factors = [jnp.exp2(top - row_top) for top in tops]
        total = factors[0] * totals[0]
        centre = factors[0] * centres[0]
        for n in range(1, len(factors)):
            total = total + factors[n] * totals[n]
            centre = centre + factors[n] * centres[n]
        inv = 1.0 / total
        centre = centre * inv
        factors = [factor * inv for factor in factors]
        out_t = None
        qgrad_t = None
        for j in range(8):
            lows, grads = [], []
            for n in range(256 // PART):
                part = slice(n * PART, (n + 1) * PART)
                probs = s_scr[slot, j, part] * factors[j * (256 // PART) + n]
                grads.append((probs * (d_scr[slot, j, part] - centre)).astype(BF16))
                lows.append(probs.astype(BF16))
            probs_low = jnp.concatenate(lows, axis=0)
            score_grad = jnp.concatenate(grads, axis=0)
            dv = dot(probs_low, dog, NN)
            dk = dot(score_grad, qg, NN)
            if g == 0:
                gacc[j, 1] = dv
                gacc[j, 0] = dk
            else:
                gacc[j, 1] += dv
                gacc[j, 0] += dk
            out_j = dot(kv[h, j, 1], probs_low, TN)
            qgrad_j = dot(kv[h, j, 0], score_grad, TN)
            out_t = out_j if out_t is None else out_t + out_j
            qgrad_t = qgrad_j if qgrad_t is None else qgrad_t + qgrad_j
        ob[h, :, :, lanes] = out_t.T.astype(BF16).reshape(2, SPAN, HD)
        qgb[h, :, :, lanes] = (qgrad_t * SCALING).T.astype(BF16).reshape(2, SPAN, HD)
        between(g)


def kernel(
    rp_ref, q_ref, do_ref, rk_ref, rv_ref, pk_ref, pv_ref,
    o_ref, qg_ref, rkg_ref, rvg_ref, pkg_ref, pvg_ref,
    qb, db, kv, stage, relay, sel, gacc, st, sr, ob, qgb, ar, zs, zr, fo, fr, gr, mb, racc, s_scr, d_scr,
    r_s, r_z, r_p, r_kv, r_q, r_d, r_o, r_qg, r_g, r_m, r_a, r_zz, r_f,
    s_z, s_p, s_kv, s_w, s_q, s_d, s_o, s_qg, s_g, s_a, s_zz, s_f,
):
    seq = lax.axis_index("seq")
    resp = lax.axis_index("resp")
    x_lo = seq // 16
    z = (seq // 2) % 8
    core = seq % 2
    chip = z % 4
    z_hi = z // 4
    plane = resp * 2 + x_lo
    head_core = resp // 4
    own_half = core == head_core

    def seq_of(x, zz, k):
        return x * 16 + zz * 2 + k

    def device(s, r):
        return {"seq": s, "resp": r}

    def remote(src, dst, send, recv, s, r):
        return pltpu.make_async_remote_copy(
            src_ref=src, dst_ref=dst, send_sem=send, recv_sem=recv,
            device_id=device(s, r), device_id_type=MESH,
        )

    def wait_for(ref, sem):
        pltpu.make_async_copy(ref, ref, sem).wait()

    def cols(start, width):
        return pl.ds(pl.multiple_of(start, 128), width)

    mine = cols(resp * HD, HD)
    for which, src in enumerate((pk_ref, pv_ref)):
        pltpu.make_async_copy(src.at[:, :, mine], stage.at[which], r_s).start()

    barrier = pltpu.get_barrier_semaphore()

    def greet(s, r):
        pl.semaphore_signal(barrier, inc=1, device_id=device(s, r), device_id_type=MESH)

    place = resp * 4 + x_lo * 2 + core

    def greet_plane(t, _):
        other = (place + t) % 32
        greet(seq_of((other // 2) % 2, z, other % 2), other // 4)
        return 0

    lax.fori_loop(1, 32, greet_plane, 0)

    def greet_line(t, _):
        greet(seq_of(x_lo, (z + t) % 8, core), resp)
        return 0

    lax.fori_loop(1, 8, greet_line, 0)

    def greet_group(t, _):
        greet(seq_of(x_lo, z_hi * 4 + (chip + t) % 4, 1 - core), resp)
        return 0

    lax.fori_loop(1, 4, greet_group, 0)

    for d in range(1, 4):

        @pl.when(chip < d)
        def _():
            for h in range(4):
                kv[h, 4 + d] = jnp.zeros((2, 256, HD), BF16)

    pl.semaphore_wait(barrier, 41)

    wait_for(stage, r_s)
    pltpu.make_async_copy(stage, relay.at[z], r_z).start()

    def send_line(t, _):
        remote(stage, relay.at[z], s_z, r_z, seq_of(x_lo, (z + t) % 8, core), resp).start()
        return 0

    lax.fori_loop(1, 8, send_line, 0)

    y = resp // 2
    x_hi = resp % 2

    def head_at(step, k):
        odd = (y + step // 2) % 2
        away = ((y - 2 * k - odd + 4) % 4) // 2
        return odd * 2 + (x_hi + step + away) % 2

    def send_inputs(step):
        h = head_at(step, core)
        h_other = head_at(step, 1 - core)
        own = cols((core * 4 + h) * 512, 512)
        other = cols(((1 - core) * 4 + h_other) * 512, 512)
        sibling = seq_of(x_lo, z, 1 - core)
        for src, dst, send, recv in ((q_ref, qb, s_q, r_q), (do_ref, db, s_d, r_d)):
            remote(
                src.at[:, other], dst.at[h_other, core], send, recv.at[h_other], sibling, resp
            ).start()
            pltpu.make_async_copy(src.at[:, own], dst.at[h, core], recv.at[h]).start()
        rows = pl.ds(pl.multiple_of(core * SPAN, SPAN), SPAN)
        for which, src in enumerate((rk_ref, rv_ref)):
            own = cols((core * 4 + h) * HD, HD)
            other = cols(((1 - core) * 4 + h_other) * HD, HD)
            pltpu.make_async_copy(
                src.at[:, own], kv.at[h, 4, which, rows], r_kv.at[h, 0]
            ).start()
            remote(
                src.at[:, other], kv.at[h_other, 4, which, rows],
                s_kv.at[0], r_kv.at[h_other, 0], sibling, resp,
            ).start()
        send_keys(step, 1)

    def sends_to(d):
        return (chip + d <= 3) if d != 2 else (chip == 0)

    def send_keys(step, d):
        rows = pl.ds(pl.multiple_of(core * SPAN, SPAN), SPAN)

        @pl.when(sends_to(d))
        def _():
            for k in range(2):
                to = head_at(step, k)
                for which, src in enumerate((rk_ref, rv_ref)):
                    remote(
                        src.at[:, cols((k * 4 + to) * HD, HD)],
                        kv.at[to, 4 + d, which, rows],
                        s_kv.at[d], r_kv.at[to, d],
                        seq_of(x_lo, z + d, k), resp,
                    ).start()

    def hand_on(step):
        h = head_at(step, core)

        @pl.when(chip == 2)
        def _():
            wait_for(kv.at[h, 5], r_kv.at[h, 1])
            remote(
                kv.at[h, 5], kv.at[h, 6], s_w, r_kv.at[h, 2], seq_of(x_lo, z + 1, core), resp
            ).start()

    def merge(step):
        h = head_at(step, core)

        @pl.when(chip == 2)
        def _():
            wait_for(mb.at[h], r_m.at[h])
            sr[h, 1] = (sr[h, 1].astype(F32) + mb[h].astype(F32)).astype(BF16)
            for k in range(2):
                remote(
                    sr.at[h, 1, k], gr.at[1, core * 4 + h], s_g.at[1], r_g.at[1],
                    seq_of(x_lo, z - 1, k), resp,
                ).start()

    send_inputs(0)

    wait_for(relay, r_z)
    quarter = x_lo * 2 + core

    def send_plane(step):
        shift = 2 * (step % 2) + step // 2
        for hi in range(2):
            for xl in range(2):
                r = ((y + shift + 2 * hi) % 4) * 2 + (x_hi + hi) % 2
                x = (x_lo + xl) % 2
                second = rp_ref[r * 4 + x * 2 + z_hi] == 1
                at = step * 4 + hi * 2 + xl
                for which in range(2):
                    sel[at, which] = jnp.where(
                        second,
                        relay[:, which, 1].reshape(256, HD),
                        relay[:, which, 0].reshape(256, HD),
                    )
                dst = kv.at[resp % 4, quarter]
                recv = r_p.at[resp % 4]
                here = (at == 0) & own_half

                @pl.when(here)
                def _():
                    pltpu.make_async_copy(sel.at[at], dst, recv).start()

                @pl.when(jnp.logical_not(here))
                def _():
                    remote(
                        sel.at[at], dst, s_p.at[at], recv, seq_of(x, z, head_core), r
                    ).start()

    send_plane(0)
    send_keys(0, 2)
    send_keys(0, 3)
    send_plane(1)
    send_inputs(1)
    send_keys(1, 2)
    send_keys(1, 3)
    hand_on(0)

    valid = [chip >= d for d in range(4)]

    def run_head(step, _):
        h = head_at(step, core)
        wait_for(qb.at[h], r_q.at[h])
        wait_for(db.at[h], r_d.at[h])
        for d in range(4):

            @pl.when((chip >= d) if d != 1 else (chip % 2 == 1))
            def _():
                wait_for(kv.at[h, 4 + d], r_kv.at[h, d])

        wait_for(kv.at[h, pl.ds(0, 4)], r_p.at[h])

        @pl.when(step < 2)
        def _():
            send_plane(step + 2)
            send_inputs(step + 2)
            send_keys(step + 2, 2)
            send_keys(step + 2, 3)

        def between(g):
            if g == 0:

                pass
            elif g == 1:

                @pl.when(step < 3)
                def _():
                    hand_on(step + 1)
            elif g == 2:

                @pl.when(step > 0)
                def _():
                    merge(step - 1)

        head_pass(h, valid, between, qb, db, kv, gacc, ob, qgb, s_scr, d_scr)
        head = core * 4 + h
        for which in range(2):
            for x in range(2):
                for k in range(2):
                    n = x * 2 + k
                    term = gacc[n, which]
                    st[h, n, which] = (term * SCALING if which == 0 else term).astype(BF16)
                    here = (head == resp) & (x == x_lo) & (k == core)
                    src = st.at[h, n, which]
                    dst = ar.at[plane, which]

                    @pl.when(here)
                    def _():
                        pltpu.make_async_copy(src, dst, r_a.at[which]).start()

                    @pl.when(jnp.logical_not(here))
                    def _():
                        remote(
                            src, dst, s_a.at[which, h, n], r_a.at[which], seq_of(x, z, k), head
                        ).start()

        def send_terms(d):
            for k in range(2):
                remote(
                    sr.at[h, d, k], gr.at[d, head], s_g.at[d], r_g.at[d],
                    seq_of(x_lo, z - d, k), resp,
                ).start()

        for d in range(4):

            @pl.when(chip >= d)
            def _():
                for k in range(2):
                    rows = slice(k * SPAN, (k + 1) * SPAN)
                    sr[h, d, k, 0] = (gacc[4 + d, 0, rows] * SCALING).astype(BF16)
                    sr[h, d, k, 1] = gacc[4 + d, 1, rows].astype(BF16)
                if d == 0:
                    dst = gr.at[0, head]
                    pltpu.make_async_copy(sr.at[h, 0, core], dst, r_g.at[0]).start()
                    remote(
                        sr.at[h, 0, 1 - core], dst, s_g.at[0], r_g.at[0],
                        seq_of(x_lo, z, 1 - core), resp,
                    ).start()
                elif d == 1:

                    @pl.when(chip != 2)
                    def _():
                        send_terms(d)
                elif d == 2:

                    @pl.when(chip == 2)
                    def _():
                        send_terms(d)

                    @pl.when(chip == 3)
                    def _():
                        remote(
                            sr.at[h, 2], mb.at[h], s_g.at[2], r_m.at[h],
                            seq_of(x_lo, z - 1, core), resp,
                        ).start()
                else:
                    send_terms(d)

        where = cols(head * 512, 512)
        for src, dst, send, recv in ((ob, o_ref, s_o, r_o), (qgb, qg_ref, s_qg, r_qg)):
            pltpu.make_async_copy(src.at[h, core], dst.at[:, where], recv).start()
            remote(
                src.at[h, 1 - core], dst.at[:, where], send, recv,
                seq_of(x_lo, z, 1 - core), resp,
            ).start()
        return 0

    lax.fori_loop(0, 4, run_head, 0)

    merge(3)

    second = [rp_ref[(a // 2) * 4 + (a % 2) * 2 + z_hi] == 1 for a in range(16)]

    for which in range(2):
        wait_for(ar.at[:, which], r_a.at[which])

        def sum_plane(t, _, which=which):
            to = (z + t) % 8
            rows = pl.ds(pl.multiple_of(to * 32, 32), 32)
            sums = [jnp.zeros((32, HD), F32), jnp.zeros((32, HD), F32)]
            for a in range(16):
                term = ar[a, which, rows].astype(F32)
                sums[0] += jnp.where(second[a], 0.0, term)
                sums[1] += jnp.where(second[a], term, 0.0)
            for p in range(2):
                zs[which, to, p] = sums[p].astype(BF16)

            @pl.when(t == 0)
            def _():
                pltpu.make_async_copy(zs.at[which, to], zr.at[which, z], r_zz.at[which]).start()

            @pl.when(t > 0)
            def _():
                remote(
                    zs.at[which, to], zr.at[which, z], s_zz, r_zz.at[which],
                    seq_of(x_lo, to, core), resp,
                ).start()

            return 0

        lax.fori_loop(0, 8, sum_plane, 0)

    wait_for(gr.at[0], r_g.at[0])
    racc[...] = gr[0].astype(F32)
    for d in range(1, 4):

        @pl.when(sends_to(d))
        def _():
            wait_for(gr.at[d], r_g.at[d])
            racc[...] += gr[d].astype(F32)

    for n in range(8):
        rkg_ref[:, n * HD : (n + 1) * HD] = racc[n, 0].astype(BF16)
        rvg_ref[:, n * HD : (n + 1) * HD] = racc[n, 1].astype(BF16)

    for which in range(2):
        wait_for(zr.at[which], r_zz.at[which])
        for p in range(2):
            final = zr[which, 0, p].astype(F32)
            for n in range(1, 8):
                final = final + zr[which, n, p].astype(F32)
            fo[which, p] = final.astype(BF16)
        pltpu.make_async_copy(fo.at[which], fr.at[which, resp], r_f.at[which]).start()

        def send_replica(t, _, which=which):
            remote(
                fo.at[which], fr.at[which, resp], s_f, r_f.at[which], seq, (resp + t) % 8
            ).start()
            return 0

        lax.fori_loop(1, 8, send_replica, 0)

    wait_for(o_ref, r_o)
    wait_for(qg_ref, r_qg)
    for which, dst in enumerate((pkg_ref, pvg_ref)):
        wait_for(fr.at[which], r_f.at[which])
        for n in range(8):
            dst[:, :, n * HD : (n + 1) * HD] = fr[which, n]

    wait_for(relay.at[pl.ds(0, 7)], s_z)
    for at in range(16):
        if at == 0:

            @pl.when(jnp.logical_not(own_half))
            def _():
                wait_for(sel.at[0], s_p.at[0])
        else:
            wait_for(sel.at[at], s_p.at[at])
    wait_for(kv.at[0, pl.ds(0, 2)], s_kv.at[0])
    wait_for(gr.at[0, pl.ds(0, 4)], s_g.at[0])
    for d in range(1, 4):

        @pl.when(sends_to(d))
        def _():
            wait_for(kv.at[0, pl.ds(0, 4)], s_kv.at[d])

        @pl.when(chip >= d)
        def _():
            wait_for(gr.at[0], s_g.at[d])

    @pl.when(chip == 2)
    def _():
        wait_for(kv.at[0, pl.ds(0, 4)], s_w)

    wait_for(qb.at[:, 0], s_q)
    wait_for(db.at[:, 0], s_d)
    wait_for(ob.at[:, 0], s_o)
    wait_for(qgb.at[:, 0], s_qg)
    for h in range(4):
        for n in range(4):
            here = (core * 4 + h == resp) & (n == quarter)

            @pl.when(jnp.logical_not(here))
            def _():
                for which in range(2):
                    wait_for(st.at[h, n, which], s_a.at[which, h, n])

    wait_for(zr.at[:, pl.ds(0, 7)], s_zz)
    wait_for(fr.at[:, pl.ds(0, 7)], s_f)


def finish(*refs):
    for src, dst in zip(refs[:6], refs[6:]):
        dst[...] = src[...]


def body(queries, resp_keys, resp_values, prompt_keys, prompt_values, response_prompt, out_grad):
    anywhere = pl.BlockSpec(memory_space=pl.ANY)
    vmem = pl.BlockSpec(memory_space=pltpu.VMEM)
    dma = pltpu.SemaphoreType.DMA
    rows = jax.ShapeDtypeStruct((SPAN, 4096), BF16)
    block = jax.ShapeDtypeStruct((SPAN, 1024), BF16)
    shard = jax.ShapeDtypeStruct((2, 32, 1024), BF16)
    results = pl.pallas_call(
        kernel,
        out_shape=(rows, rows, block, block, shard, shard),
        in_specs=[pl.BlockSpec(memory_space=pltpu.SMEM)] + [anywhere] * 6,
        out_specs=(anywhere, anywhere, vmem, vmem, vmem, vmem),
        scratch_shapes=[
            pltpu.VMEM((4, 2, SPAN, 512), BF16),
            pltpu.VMEM((4, 2, SPAN, 512), BF16),
            pltpu.VMEM((4, 8, 2, 256, HD), BF16),
            pltpu.VMEM((2, 2, 32, HD), BF16),
            pltpu.VMEM((8, 2, 2, 32, HD), BF16),
            pltpu.VMEM((16, 2, 256, HD), BF16),
            pltpu.VMEM((8, 2, 256, HD), F32),
            pltpu.VMEM((4, 4, 2, 256, HD), BF16),
            pltpu.VMEM((4, 4, 2, 2, SPAN, HD), BF16),
            pltpu.VMEM((4, 2, SPAN, 512), BF16),
            pltpu.VMEM((4, 2, SPAN, 512), BF16),
            pltpu.VMEM((16, 2, 256, HD), BF16),
            pltpu.VMEM((2, 8, 2, 32, HD), BF16),
            pltpu.VMEM((2, 8, 2, 32, HD), BF16),
            pltpu.VMEM((2, 2, 32, HD), BF16),
            pltpu.VMEM((2, 8, 2, 32, HD), BF16),
            pltpu.VMEM((4, 8, 2, SPAN, HD), BF16),
            pltpu.VMEM((4, 2, 2, SPAN, HD), BF16),
            pltpu.VMEM((8, 2, SPAN, HD), F32),
            pltpu.VMEM((2, 8, 256, 256), F32),
            pltpu.VMEM((2, 8, 256, 256), F32),
            dma(()),
            dma(()),
            dma((4,)),
            dma((4, 4)),
            dma((4,)),
            dma((4,)),
            dma(()),
            dma(()),
            dma((4,)),
            dma((4,)),
            dma((2,)),
            dma((2,)),
            dma((2,)),
            dma(()),
            dma((16,)),
            dma((4,)),
            dma(()),
            dma(()),
            dma(()),
            dma(()),
            dma(()),
            dma((4,)),
            dma((2, 4, 4)),
            dma(()),
            dma(()),
        ],
        compiler_params=pltpu.CompilerParams(
            collective_id=0, has_side_effects=True, vmem_limit_bytes=56 * 1024 * 1024
        ),
        name="attention_step",
    )(
        response_prompt, queries[0], out_grad[0], resp_keys[0], resp_values[0],
        prompt_keys, prompt_values,
    )
    parts = (
        [pl.BlockSpec((SPAN, 1024), lambda i: (0, i))] * 2
        + [pl.BlockSpec((SPAN, 256), lambda i: (0, i))] * 2
        + [pl.BlockSpec((2, 32, 256), lambda i: (0, 0, i))] * 2
    )
    attended, query_grad, rkg, rvg, pkg, pvg = pl.pallas_call(
        finish,
        out_shape=(rows, rows, block, block, shard, shard),
        grid=(4,),
        in_specs=parts,
        out_specs=parts,
        name="finish",
    )(*results)
    return (attended[None], query_grad[None], rkg[None], rvg[None], pkg, pvg)


def solution(mesh):
    by_row = P("resp", "seq", None)
    shared = P(None, "seq", None)
    return jax.shard_map(
        body,
        mesh=mesh,
        in_specs=(by_row, by_row, by_row, shared, shared, P(), by_row),
        out_specs=(by_row, by_row, by_row, by_row, shared, shared),
        check_vma=False,
    )
```
